32 devices in a mesh: groups: 2 (over x), row: 8 (over z, y), col: 2 (over core).
Axes of the slice: x: 2, y: 2, z: 4, core: 2. Of those that a mesh axis runs over, the one named last changes fastest.
Arguments:
- tokens: bfloat16 [768, 6144], P(('groups', 'row'), 'col'), parts along dimension 0, may hold values from -400 to 400, as said below
- norm_gain: float32 [6144], P('col'), may hold values from 0.1 to 1.9
- norm_bias: float32 [6144], P('col'), may hold values from -3 to 3
- up_weight: bfloat16 [6144, 24576], P('col', 'row'), may hold values from -0.078125 to 0.078125
- up_bias: float32 [24576], P('row'), may hold values from -3 to 3
- down_weight: bfloat16 [24576, 6144], P('row', 'col'), may hold values from -0.0390625 to 0.0390625
- down_bias: float32 [6144], P('col'), may hold values from -3 to 3
Outputs:
- mlp_out: bfloat16 [768, 6144], P(('groups', 'row'), 'col'), parts along dimension 0
The draws below stay inside these ranges and needn't reach their ends.
There are 2 independent parts, one for each index of `groups`. The reference program is written for one: setup_inputs(seed, part) draws one part's arguments, and reference() takes and returns one part's arrays. A program takes and returns all parts, laid end to end along the dimension named above; an argument that names none is the same for every part. Nothing has to cross between parts.
Inputs may be any that keep to these rules, and one draw needn't show every extreme that they name: Activations with a spread of scales over tokens and features.
All inputs are finite; a program needn't handle non-finite values.
Results may differ from the reference program's by a relative error of at most 0.015.
Values may be sent and summed in bfloat16 or wider, within the bound.
A program may use at most 128 MiB of HBM per device.

```python
import math
import jax
import jax.numpy as jnp
from jax import lax

D = 6144
FF = 24576
TOKENS = 384
N_ROW = 8


def draw_tokens(key, part):
    key = jax.random.fold_in(key, 11)
    first, second, third, fourth = jax.random.split(key, 4)
    row_scale = jnp.exp(jax.random.uniform(first, (TOKENS, 1), jnp.float32) * math.log(10.0))
    place = jnp.arange(D, dtype=jnp.float32) / D
    ramp = jnp.exp(place * math.log(3.0))
    col_scale = ramp[None, :] * jnp.exp(jax.random.uniform(second, (1, D), jnp.float32) * math.log(2.0))
    base = jnp.clip(jax.random.normal(third, (TOKENS, D), jnp.float32), -4.0, 4.0)
    offset = jnp.clip(jax.random.normal(fourth, (TOKENS, 1), jnp.float32), -2.0, 2.0)
    lift = jnp.exp(place * math.log(6.0))
    return (row_scale * (offset * lift[None, :] + col_scale * base)).astype(jnp.bfloat16)


def steps_of(key, extent, pieces, least, high):
    level = 1.0
    for position, shards_of in pieces:
        draws = jax.random.uniform(jax.random.fold_in(jax.random.fold_in(key, 6), position), (shards_of,), jnp.float32, least / len(pieces), high / len(pieces))
        level = level * jnp.repeat(jnp.exp(draws), extent[position] // shards_of).reshape((-1,) + (1,) * (len(extent) - 1 - position))
    return level


def scatter_about(rng, extent, spread, limit, pieces=(), kind=jnp.bfloat16):
    values = spread * jax.random.normal(rng, extent, jnp.float32)
    if pieces:
        values = values * steps_of(rng, extent, pieces, -0.22, 0.18)
    return jnp.clip(values, -limit, limit).astype(kind)


def setup_inputs(seed: int = 0, part: int = 0) -> dict:
    arg_keys = jax.random.split(jax.random.key(seed), 8)
    part_keys = jax.random.split(jax.random.fold_in(arg_keys[7], part), 8)
    tokens = draw_tokens(jax.random.fold_in(jax.random.fold_in(arg_keys[7], part), 71), part)
    norm_gain = jnp.clip(1.0 + 0.18 * jax.random.normal(arg_keys[1], (D,), jnp.float32), 0.1, 1.9)
    norm_bias = scatter_about(arg_keys[2], (D,), 0.5, 3.0, ((0, 2),), jnp.float32)
    up_weight = scatter_about(arg_keys[3], (D, FF), D ** -0.5, 0.078125, ((0, 2), (1, 8)))
    up_bias = scatter_about(arg_keys[4], (FF,), 0.5, 3.0, ((0, 8),), jnp.float32)
    down_weight = scatter_about(arg_keys[5], (FF, D), FF ** -0.5, 0.0390625, ((0, 8), (1, 2)))
    down_bias = scatter_about(arg_keys[6], (D,), 0.5, 3.0, ((0, 2),), jnp.float32)
    return {"tokens": tokens, "norm_gain": norm_gain, "norm_bias": norm_bias, "up_weight": up_weight, "up_bias": up_bias, "down_weight": down_weight, "down_bias": down_bias}


def reference(tokens, norm_gain, norm_bias, up_weight, up_bias, down_weight, down_bias):
    values = tokens.astype(jnp.float32)
    mean = lax.optimization_barrier(jnp.sum(values, axis=1, keepdims=True)) / D
    deviation = values - mean
    variance = lax.optimization_barrier(jnp.sum(deviation * deviation, axis=1, keepdims=True)) / D
    normed = (deviation * lax.rsqrt(variance + 1e-05) * norm_gain + norm_bias).astype(jnp.bfloat16)
    pre = jnp.dot(normed, up_weight, preferred_element_type=jnp.float32) + up_bias
    hidden = jax.nn.gelu(pre, approximate=True).astype(jnp.bfloat16)
    block = FF // N_ROW

    def add_block(index, total):
        start = (index * block).astype(jnp.int32)
        units = lax.dynamic_slice_in_dim(hidden, start, block, 1)
        rows = lax.dynamic_slice_in_dim(down_weight, start, block, 0)
        term = jnp.dot(units, rows, preferred_element_type=jnp.float32).astype(jnp.bfloat16)
        term = lax.optimization_barrier(term)
        return total + term.astype(jnp.float32)
    total = lax.fori_loop(jnp.int32(0), jnp.int32(N_ROW), add_block, jnp.zeros((hidden.shape[0], D), jnp.float32))
    return (total + down_bias).astype(jnp.bfloat16)
```

```python
import functools

import jax
import jax.numpy as jnp
from jax import lax
from jax.experimental import pallas as pl
from jax.experimental.pallas import tpu as pltpu
from jax.sharding import PartitionSpec as P

MESH = pl.DeviceIdType.MESH
F32 = jnp.float32
BF16 = jnp.bfloat16


def kernel(
    nz, ny,
    tok_ref, gain_ref, nbias_ref, w1_hbm, ubias_ref, w2_hbm, dbias_ref, out_ref,
    w1, w2, x_all, ppart, psend, precv, hidden, pout, yrecv, zrecv, stat, stat_in,
    w_sem, st_sem, x_recv, x_up, x_dn, x_y, p_s, p_r, y_s, y_r, z_s, z_r,
):
    r = lax.axis_index("row")
    c = lax.axis_index("col")
    z, y = r // ny, r % ny
    t, dh = tok_ref.shape
    ff = w1.shape[1]
    rows = ny * t
    wide = 512 if ff % 512 == 0 else 256
    core = {"col": 1 - c}

    def row_of(level, column):
        return level * ny + column

    def remote(src, dst, s_sem, r_sem, device):
        return pltpu.make_async_remote_copy(
            src_ref=src, dst_ref=dst, send_sem=s_sem, recv_sem=r_sem,
            device_id=device, device_id_type=MESH,
        )

    load1 = pltpu.make_async_copy(w1_hbm, w1, w_sem.at[0])
    load2 = pltpu.make_async_copy(w2_hbm, w2, w_sem.at[1])
    load1.start()
    load2.start()

    x = tok_ref[...].astype(F32)
    mean_here = jnp.sum(x, axis=1, keepdims=True) / dh
    dev = x - mean_here
    m2_here = jnp.sum(dev * dev, axis=1, keepdims=True)
    stat[0] = jnp.broadcast_to(mean_here, (t, 128))
    stat[1] = jnp.broadcast_to(m2_here, (t, 128))

    barrier = pltpu.get_barrier_semaphore()
    pl.semaphore_signal(barrier, inc=1, device_id=core, device_id_type=MESH)
    if ny == 2:
        pl.semaphore_signal(
            barrier, inc=1, device_id={"row": row_of(z, 1 - y)}, device_id_type=MESH
        )

    @pl.when(z > 0)
    def _():
        pl.semaphore_signal(
            barrier, inc=1, device_id={"row": row_of(z - 1, y)}, device_id_type=MESH
        )

    @pl.when(z < nz - 1)
    def _():
        pl.semaphore_signal(
            barrier, inc=1, device_id={"row": row_of(z + 1, y)}, device_id_type=MESH
        )

    pl.semaphore_wait(barrier, ny + jnp.where(z > 0, 1, 0) + jnp.where(z < nz - 1, 1, 0))

    swap = remote(stat, stat_in, st_sem.at[0], st_sem.at[1], core)
    swap.start()
    swap.wait()
    other_mean = stat_in[0][:, :1]
    other_m2 = stat_in[1][:, :1]
    gap = mean_here - other_mean
    mean = 0.5 * (mean_here + other_mean)
    var = (m2_here + other_m2 + (0.5 * dh) * gap * gap) / (2 * dh)
    x_all[r] = (
        (tok_ref[...].astype(F32) - mean) * lax.rsqrt(var + 1e-05) * gain_ref[...] + nbias_ref[...]
    ).astype(BF16)

    def x_copy(level, sems, device_row):
        slot = row_of(level, y)
        return remote(
            x_all.at[slot], x_all.at[slot], sems.at[level], x_recv.at[slot], {"row": device_row}
        )

    def up_copy(level):
        return x_copy(level, x_up, row_of(z + 1, y))

    def dn_copy(level):
        return x_copy(level, x_dn, row_of(z - 1, y))

    def y_copy(level):
        return x_copy(level, x_y, row_of(z, 1 - y))

    def x_wait(slot):
        remote(
            x_all.at[slot], x_all.at[slot], x_up.at[0], x_recv.at[slot], core
        ).wait_recv()

    def p_copy(level):
        return remote(psend.at[level], precv.at[level], p_s.at[level], p_r.at[level], core)

    def process(level):
        if ny == 2:
            x_wait(row_of(level, 1 - y))

        @pl.loop(0, ff // wide)
        def _(j):
            cols = pl.ds(pl.multiple_of(j * wide, wide), wide)
            block = x_all[pl.ds(level * ny, ny)].reshape(rows, dh)
            value = jnp.dot(block, w1[:, cols], preferred_element_type=F32)
            ppart[level, :, cols] = value
            psend[level, :, cols] = value.astype(BF16)

        p_copy(level).start()

    def finish(level):
        p_copy(level).wait_recv()

        @pl.loop(0, ff // wide)
        def _(j):
            cols = pl.ds(pl.multiple_of(j * wide, wide), wide)
            pre = ppart[level, :, cols] + precv[level, :, cols].astype(F32) + ubias_ref[:, cols]
            hidden[level, :, cols] = jax.nn.gelu(pre, approximate=True).astype(BF16)

    def each_at(d, act):
        @pl.when((d >= 0) & (z - d >= 0))
        def _():
            act(z - d)

        @pl.when((d > 0) & (z + d <= nz - 1))
        def _():
            act(z + d)

    @pl.loop(0, nz + 2)
    def _(s):
        @pl.when((s > 0) & (z - s >= 0))
        def _():
            x_wait(row_of(z - s, y))

        @pl.when((s < nz) & (z - s >= 0) & (z < nz - 1))
        def _():
            up_copy(z - s).start()

        if ny == 2:
            @pl.when((s < nz) & (z - s >= 0))
            def _():
                y_copy(z - s).start()

        @pl.when((s > 0) & (z + s <= nz - 1))
        def _():
            x_wait(row_of(z + s, y))

        @pl.when((s < nz) & (z + s <= nz - 1) & (z > 0))
        def _():
            dn_copy(z + s).start()

        if ny == 2:
            @pl.when((s > 0) & (z + s <= nz - 1))
            def _():
                y_copy(z + s).start()

        @pl.when(s == 1)
        def _():
            load1.wait()

        each_at(s - 1, process)
        each_at(s - 2, finish)

    load2.wait()

    def yp_copy(level):
        return remote(
            pout.at[row_of(level, 1 - y)], yrecv.at[level], y_s.at[level], y_r.at[level],
            {"row": row_of(z, 1 - y)},
        )

    def project(level):
        @pl.loop(0, dh // wide)
        def _(j):
            cols = pl.ds(pl.multiple_of(j * wide, wide), wide)
            value = jnp.dot(hidden[level], w2[:, cols], preferred_element_type=F32)
            pout[pl.ds(level * ny, ny), :, cols] = value.astype(BF16).reshape(ny, t, wide)

        if ny == 2:
            yp_copy(level).start()

    def zd_copy(level):
        slot = jnp.where(z - 1 == level, nz, level)
        return remote(
            pout.at[row_of(level, y)], zrecv.at[slot], z_s.at[level], z_r.at[slot],
            {"row": row_of(z - 1, y)},
        )

    def zu_copy(level):
        return remote(
            pout.at[row_of(level, y)], zrecv.at[level], z_s.at[level], z_r.at[level],
            {"row": row_of(z + 1, y)},
        )

    def z_wait(slot):
        remote(
            zrecv.at[slot], zrecv.at[slot], z_s.at[0], z_r.at[slot], core
        ).wait_recv()

    def reduce(level):
        slot = row_of(level, y)
        inner = ((level < z) & (z < nz - 1)) | ((level > z) & (z > 0))
        if ny == 2:
            yp_copy(level).wait_recv()

        @pl.when(inner)
        def _():
            z_wait(level)
            total = pout[slot].astype(F32) + zrecv[level].astype(F32)
            if ny == 2:
                total += yrecv[level].astype(F32)
            pout[slot] = total.astype(BF16)

        if ny == 2:
            @pl.when(jnp.logical_not(inner))
            def _():
                pout[slot] = (pout[slot].astype(F32) + yrecv[level].astype(F32)).astype(BF16)

        @pl.when(level < z)
        def _():
            zd_copy(level).start()

        @pl.when(level > z)
        def _():
            zu_copy(level).start()

    @pl.loop(0, nz)
    def _(s):
        d = nz - 1 - s
        each_at(d, project)

        @pl.when(d < nz - 1)
        def _():
            each_at(d + 1, reduce)

    if ny == 2:
        yp_copy(z).wait_recv()
    total = pout[r].astype(F32)
    if ny == 2:
        total += yrecv[z].astype(F32)
    lower = (z > 0)
    upper = (z < nz - 1)

    ppart_own = total + dbias_ref[...]

    @pl.when(lower & upper)
    def _():
        z_wait(z)
        z_wait(nz)
        out_ref[...] = (ppart_own + zrecv[z].astype(F32) + zrecv[nz].astype(F32)).astype(BF16)

    @pl.when(lower & jnp.logical_not(upper))
    def _():
        z_wait(z)
        out_ref[...] = (ppart_own + zrecv[z].astype(F32)).astype(BF16)

    @pl.when(upper & jnp.logical_not(lower))
    def _():
        z_wait(nz)
        out_ref[...] = (ppart_own + zrecv[nz].astype(F32)).astype(BF16)

    @pl.loop(0, nz)
    def _(level):
        @pl.when((level <= z) & (z < nz - 1))
        def _():
            up_copy(level).wait_send()

        @pl.when((level >= z) & (z > 0))
        def _():
            dn_copy(level).wait_send()

        if ny == 2:
            y_copy(level).wait_send()
            yp_copy(level).wait_send()
        p_copy(level).wait_send()

        @pl.when(level != z)
        def _():
            zu_copy(level).wait_send()


def solution(mesh):
    n_row = mesh.shape["row"]
    ny = 2 if n_row == 8 else 1
    nz = n_row // ny

    def on_device(tokens, norm_gain, norm_bias, up_weight, up_bias, down_weight, down_bias):
        t, dh = tokens.shape
        ff = up_weight.shape[1]
        dout = down_weight.shape[1]
        vmem = pl.BlockSpec(memory_space=pltpu.VMEM)
        hbm = pl.BlockSpec(memory_space=pl.ANY)
        dma = pltpu.SemaphoreType.DMA
        rows = ny * t
        return pl.pallas_call(
            functools.partial(kernel, nz, ny),
            out_shape=jax.ShapeDtypeStruct((t, dout), BF16),
            in_specs=[vmem, vmem, vmem, hbm, vmem, hbm, vmem],
            out_specs=vmem,
            scratch_shapes=[
                pltpu.VMEM((dh, ff), BF16),
                pltpu.VMEM((ff, dout), BF16),
                pltpu.VMEM((n_row, t, dh), BF16),
                pltpu.VMEM((nz, rows, ff), F32),
                pltpu.VMEM((nz, rows, ff), BF16),
                pltpu.VMEM((nz, rows, ff), BF16),
                pltpu.VMEM((nz, rows, ff), BF16),
                pltpu.VMEM((n_row, t, dout), BF16),
                pltpu.VMEM((nz if ny == 2 else 1, t, dout), BF16),
                pltpu.VMEM((nz + 1, t, dout), BF16),
                pltpu.VMEM((2, t, 128), F32),
                pltpu.VMEM((2, t, 128), F32),
                dma((2,)), dma((2,)), dma((n_row,)),
                dma((nz,)), dma((nz,)), dma((nz,)),
                dma((nz,)), dma((nz,)), dma((nz,)), dma((nz,)),
                dma((nz,)), dma((nz + 1,)),
            ],
            compiler_params=pltpu.CompilerParams(
                collective_id=0, has_side_effects=True, vmem_limit_bytes=62 * 1024 * 1024
            ),
            cost_estimate=pl.CostEstimate(
                flops=4 * n_row * t * dh * ff, bytes_accessed=4 * dh * ff, transcendentals=0
            ),
        )(
            tokens, norm_gain.reshape(1, -1), norm_bias.reshape(1, -1), up_weight,
            up_bias.reshape(1, -1), down_weight, down_bias.reshape(1, -1),
        )

    in_specs = (
        P(("groups", "row"), "col"),
        P("col"),
        P("col"),
        P("col", "row"),
        P("row"),
        P("row", "col"),
        P("col"),
    )
    out_specs = P(("groups", "row"), "col")
    return jax.shard_map(
        on_device, mesh=mesh, in_specs=in_specs, out_specs=out_specs, check_vma=False
    )
```

```python
import functools

import jax
import jax.numpy as jnp
from jax import lax
from jax.experimental import pallas as pl
from jax.experimental.pallas import tpu as pltpu
from jax.sharding import PartitionSpec as P

MESH = pl.DeviceIdType.MESH
F32 = jnp.float32
BF16 = jnp.bfloat16


def kernel(
    nz, ny,
    tok_ref, gain_ref, nbias_ref, w1_hbm, ubias_ref, w2_hbm, dbias_ref, out_ref,
    w1, w2, x_all, ppart, psend, precv, hidden, pout, yrecv, zrecv, zside, acc, stat, stat_in,
    w_sem, st_sem, x_recv, x_up, x_dn, x_y, p_s, p_r, y_s, y_r, z_s, z_r,
):
    r = lax.axis_index("row")
    c = lax.axis_index("col")
    z, y = r // ny, r % ny
    t, dh = tok_ref.shape
    ff = w1.shape[1]
    rows = ny * t
    wide = 1024 if ff % 1024 == 0 else 256
    core = {"col": 1 - c}

    def row_of(level, column):
        return level * ny + column

    def remote(src, dst, s_sem, r_sem, device):
        return pltpu.make_async_remote_copy(
            src_ref=src, dst_ref=dst, send_sem=s_sem, recv_sem=r_sem,
            device_id=device, device_id_type=MESH,
        )

    load1 = pltpu.make_async_copy(w1_hbm, w1, w_sem.at[0])
    load2 = pltpu.make_async_copy(w2_hbm, w2, w_sem.at[1])
    load1.start()
    load2.start()

    x = tok_ref[...].astype(F32)
    mean_here = jnp.sum(x, axis=1, keepdims=True) / dh
    dev = x - mean_here
    m2_here = jnp.sum(dev * dev, axis=1, keepdims=True)
    stat[0] = jnp.broadcast_to(mean_here, (t, 128))
    stat[1] = jnp.broadcast_to(m2_here, (t, 128))

    barrier = pltpu.get_barrier_semaphore()
    pl.semaphore_signal(barrier, inc=1, device_id=core, device_id_type=MESH)
    if ny == 2:
        pl.semaphore_signal(
            barrier, inc=1, device_id={"row": row_of(z, 1 - y)}, device_id_type=MESH
        )

    @pl.when(z > 0)
    def _():
        pl.semaphore_signal(
            barrier, inc=1, device_id={"row": row_of(z - 1, y)}, device_id_type=MESH
        )

    @pl.when(z < nz - 1)
    def _():
        pl.semaphore_signal(
            barrier, inc=1, device_id={"row": row_of(z + 1, y)}, device_id_type=MESH
        )

    pl.semaphore_wait(barrier, ny + jnp.where(z > 0, 1, 0) + jnp.where(z < nz - 1, 1, 0))

    swap = remote(stat, stat_in, st_sem.at[0], st_sem.at[1], core)
    swap.start()
    swap.wait()
    other_mean = stat_in[0][:, :1]
    other_m2 = stat_in[1][:, :1]
    gap = mean_here - other_mean
    mean = 0.5 * (mean_here + other_mean)
    var = (m2_here + other_m2 + (0.5 * dh) * gap * gap) / (2 * dh)
    x_all[r] = (
        (tok_ref[...].astype(F32) - mean) * lax.rsqrt(var + 1e-05) * gain_ref[...] + nbias_ref[...]
    ).astype(BF16)

    edges = (0, dh // 6, dh // 2, dh)
    cut = [pl.ds(edges[k], edges[k + 1] - edges[k]) for k in range(3)]
    plain = (1, 2) if ny == 2 else (1, 2, 0)

    def x_copy(slot, k, sems, device_row):
        part = x_all.at[slot, :, cut[k]]
        return remote(part, part, sems.at[slot, k], x_recv.at[slot, k], {"row": device_row})

    def up_copy(slot, k):
        return x_copy(slot, k, x_up, row_of(z + 1, y))

    def dn_copy(slot, k):
        return x_copy(slot, k, x_dn, row_of(z - 1, y))

    def y_copy(slot, k):
        return x_copy(slot, k, x_y, row_of(z, 1 - y))

    def x_wait(slot, k):
        x_copy(slot, k, x_up, r).wait_recv()

    def p_copy(level):
        return remote(psend.at[level], precv.at[level], p_s.at[level], p_r.at[level], core)

    def process(level):
        if ny == 2:
            for k in plain:
                x_wait(row_of(level, 1 - y), k)

        @pl.loop(0, ff // wide)
        def _(j):
            cols = pl.ds(pl.multiple_of(j * wide, wide), wide)
            block = x_all[pl.ds(level * ny, ny)].reshape(rows, dh)
            value = jnp.dot(block, w1[:, cols], preferred_element_type=F32)
            ppart[level, :, cols] = value
            psend[level, :, cols] = value.astype(BF16)

        p_copy(level).start()

    def finish(level):
        p_copy(level).wait_recv()

        @pl.loop(0, ff // wide)
        def _(j):
            cols = pl.ds(pl.multiple_of(j * wide, wide), wide)
            pre = ppart[level, :, cols] + precv[level, :, cols].astype(F32) + ubias_ref[:, cols]
            hidden[level, :, cols] = jax.nn.gelu(pre, approximate=True).astype(BF16)

    def yp_copy(level, k):
        return remote(
            pout.at[row_of(level, 1 - y), :, cut[k]], yrecv.at[level, :, cut[k]],
            y_s.at[level, k], y_r.at[level, k], {"row": row_of(z, 1 - y)},
        )

    def send_y(level):
        if ny == 2:
            for k in plain:
                yp_copy(level, k).start()

    def project(level):
        step = 512 if edges[1] % 512 == 0 else 128
        for k in (1, 2, 0):
            @pl.loop(edges[k] // step, edges[k + 1] // step)
            def _(j):
                cols = pl.ds(pl.multiple_of(j * step, step), step)
                value = jnp.dot(hidden[level], w2[:, cols], preferred_element_type=F32)
                pout[pl.ds(level * ny, ny), :, cols] = value.astype(BF16).reshape(ny, t, step)

            if ny == 2 and k in plain:
                @pl.when(is_far(level))
                def _():
                    yp_copy(level, k).start()

    def is_far(level):
        return (z - level >= nz - 2) | (level - z >= nz - 2)

    def each_at(d, act):
        @pl.when((d >= 0) & (z - d >= 0))
        def _():
            act(z - d)

        @pl.when((d > 0) & (z + d <= nz - 1))
        def _():
            act(z + d)

    below_ok = z > 0
    above_ok = z < nz - 1

    if ny == 2:
        y_copy(r, 0).start()
    for k in (1, 2, 0):
        @pl.when(above_ok)
        def _():
            up_copy(r, k).start()

        @pl.when(below_ok)
        def _():
            dn_copy(r, k).start()

        if ny == 2 and k in plain:
            y_copy(r, k).start()
    if ny == 2:
        mate = row_of(z, 1 - y)
        x_wait(mate, 0)

        @pl.when(above_ok)
        def _():
            up_copy(mate, 0).start()

        @pl.when(below_ok)
        def _():
            dn_copy(mate, 0).start()

    def relay(s, column, k, cross):
        @pl.when(z - s >= 0)
        def _():
            slot = row_of(z - s, column)
            x_wait(slot, k)

            @pl.when(above_ok)
            def _():
                up_copy(slot, k).start()

            if cross:
                y_copy(slot, k).start()

        @pl.when(z + s <= nz - 1)
        def _():
            slot = row_of(z + s, column)
            x_wait(slot, k)

            @pl.when(below_ok)
            def _():
                dn_copy(slot, k).start()

            if cross:
                y_copy(slot, k).start()

    load1.wait()

    @pl.loop(1, nz + 1)
    def _(s):
        @pl.when(s < nz)
        def _():
            for k in plain:
                relay(s, y, k, ny == 2)
            if ny == 2:
                relay(s, y, 0, False)
                relay(s, 1 - y, 0, False)

        each_at(s - 1, process)

        @pl.when(s == 1)
        def _():
            load2.wait()

        each_at(s - 1, finish)
        each_at(s - 1, project)

    @pl.loop(0, nz)
    def _(i):
        def late(level):
            @pl.when(jnp.logical_not(is_far(level)))
            def _():
                send_y(level)

        each_at(nz - 1 - i, late)

    def zd_copy(level, k):
        slot = jnp.where(z - 1 == level, nz, level)
        return z_copy(level, slot, k, row_of(z - 1, y))

    def zu_copy(level, k):
        return z_copy(level, level, k, row_of(z + 1, y))

    def z_copy(level, slot, k, device_row):
        if k == 3:
            src, dst = pout.at[row_of(level, 1 - y), :, cut[0]], zside.at[slot]
        else:
            src, dst = pout.at[row_of(level, y), :, cut[k]], zrecv.at[slot, :, cut[k]]
        return remote(src, dst, z_s.at[level, k], z_r.at[slot, k], {"row": device_row})

    def z_wait(slot, k):
        level = jnp.where(slot == nz, 0, slot)
        z_copy(level, slot, k, r).wait_recv()

    def incoming(slot, k):
        return zside[slot] if k == 3 else zrecv[slot, :, cut[k]]

    def reduce(level):
        inner = ((level < z) & above_ok) | ((level > z) & below_ok)
        order = (0, 3, 1, 2) if ny == 2 else plain
        for k in order:
            slot = row_of(level, 1 - y if k == 3 else y)
            where = cut[0] if k == 3 else cut[k]
            crossed = ny == 2 and k in plain
            if crossed:
                yp_copy(level, k).wait_recv()

            @pl.when(inner)
            def _():
                z_wait(level, k)
                total = pout[slot, :, where].astype(F32) + incoming(level, k).astype(F32)
                if crossed:
                    total += yrecv[level, :, where].astype(F32)
                pout[slot, :, where] = total.astype(BF16)

            if crossed:
                @pl.when(jnp.logical_not(inner))
                def _():
                    pout[slot, :, where] = (
                        pout[slot, :, where].astype(F32) + yrecv[level, :, where].astype(F32)
                    ).astype(BF16)

            @pl.when(level < z)
            def _():
                zd_copy(level, k).start()

            @pl.when(level > z)
            def _():
                zu_copy(level, k).start()

    @pl.loop(0, nz - 1)
    def _(i):
        each_at(nz - 1 - i, reduce)

    def settle(k):
        slot = row_of(z, 1 - y) if k == 3 else r
        where = cut[0] if k == 3 else cut[k]
        acc[:, where] = pout[slot, :, where].astype(F32)

        @pl.when(below_ok)
        def _():
            z_wait(z, k)
            acc[:, where] += incoming(z, k).astype(F32)

        @pl.when(above_ok)
        def _():
            z_wait(nz, k)
            acc[:, where] += incoming(nz, k).astype(F32)

    if ny == 2:
        settle(3)
        pout[row_of(z, 1 - y), :, cut[0]] = acc[:, cut[0]].astype(BF16)
        yp_copy(z, 0).start()
    for k in (1, 2, 0):
        settle(k)
        total = acc[:, cut[k]] + dbias_ref[:, cut[k]]
        if ny == 2:
            yp_copy(z, k).wait_recv()
            total += yrecv[z, :, cut[k]].astype(F32)
        out_ref[:, cut[k]] = total.astype(BF16)

    @pl.loop(0, nz)
    def _(level):
        slots = [(row_of(level, y), k) for k in range(3)]
        if ny == 2:
            slots.append((row_of(level, 1 - y), 0))

        @pl.when((level <= z) & above_ok)
        def _():
            for slot, k in slots:
                up_copy(slot, k).wait_send()

        @pl.when((level >= z) & below_ok)
        def _():
            for slot, k in slots:
                dn_copy(slot, k).wait_send()

        if ny == 2:
            for k in plain:
                y_copy(row_of(level, y), k).wait_send()
                yp_copy(level, k).wait_send()
        p_copy(level).wait_send()

        @pl.when(level != z)
        def _():
            for k in range(4 if ny == 2 else 3):
                zu_copy(level, k).wait_send()

    if ny == 2:
        y_copy(r, 0).wait_send()
        yp_copy(z, 0).wait_send()


def solution(mesh):
    n_row = mesh.shape["row"]
    ny = 2 if n_row == 8 else 1
    nz = n_row // ny

    def on_device(tokens, norm_gain, norm_bias, up_weight, up_bias, down_weight, down_bias):
        t, dh = tokens.shape
        ff = up_weight.shape[1]
        dout = down_weight.shape[1]
        vmem = pl.BlockSpec(memory_space=pltpu.VMEM)
        hbm = pl.BlockSpec(memory_space=pl.ANY)
        dma = pltpu.SemaphoreType.DMA
        rows = ny * t
        return pl.pallas_call(
            functools.partial(kernel, nz, ny),
            out_shape=jax.ShapeDtypeStruct((t, dout), BF16),
            in_specs=[vmem, vmem, vmem, hbm, vmem, hbm, vmem],
            out_specs=vmem,
            scratch_shapes=[
                pltpu.VMEM((dh, ff), BF16),
                pltpu.VMEM((ff, dout), BF16),
                pltpu.VMEM((n_row, t, dh), BF16),
                pltpu.VMEM((nz, rows, ff), F32),
                pltpu.VMEM((nz, rows, ff), BF16),
                pltpu.VMEM((nz, rows, ff), BF16),
                pltpu.VMEM((nz, rows, ff), BF16),
                pltpu.VMEM((n_row, t, dout), BF16),
                pltpu.VMEM((nz if ny == 2 else 1, t, dout), BF16),
                pltpu.VMEM((nz + 1, t, dout), BF16),
                pltpu.VMEM((nz + 1 if ny == 2 else 1, t, dout // 6), BF16),
                pltpu.VMEM((t, dout), F32),
                pltpu.VMEM((2, t, 128), F32),
                pltpu.VMEM((2, t, 128), F32),
                dma((2,)), dma((2,)), dma((n_row, 3)),
                dma((n_row, 3)), dma((n_row, 3)), dma((n_row, 3)),
                dma((nz,)), dma((nz,)), dma((nz, 3)), dma((nz, 3)),
                dma((nz, 4)), dma((nz + 1, 4)),
            ],
            compiler_params=pltpu.CompilerParams(
                collective_id=0, has_side_effects=True, vmem_limit_bytes=62 * 1024 * 1024
            ),
            cost_estimate=pl.CostEstimate(
                flops=4 * n_row * t * dh * ff, bytes_accessed=4 * dh * ff, transcendentals=0
            ),
        )(
            tokens, norm_gain.reshape(1, -1), norm_bias.reshape(1, -1), up_weight,
            up_bias.reshape(1, -1), down_weight, down_bias.reshape(1, -1),
        )

    in_specs = (
        P(("groups", "row"), "col"),
        P("col"),
        P("col"),
        P("col", "row"),
        P("row"),
        P("row", "col"),
        P("col"),
    )
    out_specs = P(("groups", "row"), "col")
    return jax.shard_map(
        on_device, mesh=mesh, in_specs=in_specs, out_specs=out_specs, check_vma=False
    )
```

```python
import functools

import jax
import jax.numpy as jnp
from jax import lax
from jax.experimental import pallas as pl
from jax.experimental.pallas import tpu as pltpu
from jax.sharding import PartitionSpec as P

MESH = pl.DeviceIdType.MESH
F32 = jnp.float32
BF16 = jnp.bfloat16


def kernel(
    nz, ny,
    tok_ref, gain_ref, nbias_ref, w1_hbm, ubias_ref, w2_hbm, dbias_ref, out_ref,
    w1, w2, x_all, ppart, psend, precv, hidden, pout, yrecv, zrecv, zside, acc, stat, stat_in,
    w_sem, st_sem, x_recv, x_up, x_dn, x_y, p_s, p_r, y_s, y_r, z_s, z_r,
):
    r = lax.axis_index("row")
    c = lax.axis_index("col")
    z, y = r // ny, r % ny
    t, dh = tok_ref.shape
    ff = w1.shape[1]
    rows = ny * t
    wide = ff
    core = {"col": 1 - c}

    def row_of(level, column):
        return level * ny + column

    def remote(src, dst, s_sem, r_sem, device):
        return pltpu.make_async_remote_copy(
            src_ref=src, dst_ref=dst, send_sem=s_sem, recv_sem=r_sem,
            device_id=device, device_id_type=MESH,
        )

    load1 = pltpu.make_async_copy(w1_hbm, w1, w_sem.at[0])
    load2 = pltpu.make_async_copy(w2_hbm, w2, w_sem.at[1])
    load1.start()
    load2.start()

    x = tok_ref[...].astype(F32)
    mean_here = jnp.sum(x, axis=1, keepdims=True) / dh
    dev = x - mean_here
    m2_here = jnp.sum(dev * dev, axis=1, keepdims=True)
    stat[0] = jnp.broadcast_to(mean_here, (t, 128))
    stat[1] = jnp.broadcast_to(m2_here, (t, 128))

    barrier = pltpu.get_barrier_semaphore()
    pl.semaphore_signal(barrier, inc=1, device_id=core, device_id_type=MESH)
    if ny == 2:
        pl.semaphore_signal(
            barrier, inc=1, device_id={"row": row_of(z, 1 - y)}, device_id_type=MESH
        )

    @pl.when(z > 0)
    def _():
        pl.semaphore_signal(
            barrier, inc=1, device_id={"row": row_of(z - 1, y)}, device_id_type=MESH
        )

    @pl.when(z < nz - 1)
    def _():
        pl.semaphore_signal(
            barrier, inc=1, device_id={"row": row_of(z + 1, y)}, device_id_type=MESH
        )

    pl.semaphore_wait(barrier, ny + jnp.where(z > 0, 1, 0) + jnp.where(z < nz - 1, 1, 0))

    swap = remote(stat, stat_in, st_sem.at[0], st_sem.at[1], core)
    swap.start()
    swap.wait()
    other_mean = stat_in[0][:, :1]
    other_m2 = stat_in[1][:, :1]
    gap = mean_here - other_mean
    mean = 0.5 * (mean_here + other_mean)
    var = (m2_here + other_m2 + (0.5 * dh) * gap * gap) / (2 * dh)
    x_all[r] = (
        (tok_ref[...].astype(F32) - mean) * lax.rsqrt(var + 1e-05) * gain_ref[...] + nbias_ref[...]
    ).astype(BF16)

    edges = (0, dh // 6, dh // 2, dh)
    cut = [pl.ds(edges[k], edges[k + 1] - edges[k]) for k in range(3)]
    plain = (1, 2) if ny == 2 else (1, 2, 0)

    def x_copy(slot, k, sems, device_row):
        part = x_all.at[slot, :, cut[k]]
        return remote(part, part, sems.at[slot, k], x_recv.at[slot, k], {"row": device_row})

    def up_copy(slot, k):
        return x_copy(slot, k, x_up, row_of(z + 1, y))

    def dn_copy(slot, k):
        return x_copy(slot, k, x_dn, row_of(z - 1, y))

    def y_copy(slot, k):
        return x_copy(slot, k, x_y, row_of(z, 1 - y))

    def x_wait(slot, k):
        x_copy(slot, k, x_up, r).wait_recv()

    def p_copy(level):
        return remote(psend.at[level], precv.at[level], p_s.at[level], p_r.at[level], core)

    def process(level):
        if ny == 2:
            for k in plain:
                x_wait(row_of(level, 1 - y), k)

        @pl.loop(0, ff // wide)
        def _(j):
            cols = pl.ds(pl.multiple_of(j * wide, wide), wide)
            block = x_all[pl.ds(level * ny, ny)].reshape(rows, dh)
            value = jnp.dot(block, w1[:, cols], preferred_element_type=F32)
            ppart[level, :, cols] = value
            psend[level, :, cols] = value.astype(BF16)

        p_copy(level).start()

    def finish(level):
        p_copy(level).wait_recv()

        @pl.loop(0, ff // wide)
        def _(j):
            cols = pl.ds(pl.multiple_of(j * wide, wide), wide)
            pre = ppart[level, :, cols] + precv[level, :, cols].astype(F32) + ubias_ref[:, cols]
            hidden[level, :, cols] = jax.nn.gelu(pre, approximate=True).astype(BF16)

    def yp_copy(level, k):
        return remote(
            pout.at[row_of(level, 1 - y), :, cut[k]], yrecv.at[level, :, cut[k]],
            y_s.at[level, k], y_r.at[level, k], {"row": row_of(z, 1 - y)},
        )

    def project(level):
        step = 512 if edges[1] % 512 == 0 else 128
        for k in (1, 2, 0):
            if True:
                step = edges[k + 1] - edges[k]
                cols = cut[k]
                value = jnp.dot(hidden[level], w2[:, cols], preferred_element_type=F32)
                pout[pl.ds(level * ny, ny), :, cols] = value.astype(BF16).reshape(ny, t, step)

            if ny == 2 and k in plain:
                yp_copy(level, k).start()

    def each_at(d, act):
        @pl.when((d >= 0) & (z - d >= 0))
        def _():
            act(z - d)

        @pl.when((d > 0) & (z + d <= nz - 1))
        def _():
            act(z + d)

    below_ok = z > 0
    above_ok = z < nz - 1

    if ny == 2:
        y_copy(r, 0).start()
    for k in (1, 2, 0):
        @pl.when(above_ok)
        def _():
            up_copy(r, k).start()

        @pl.when(below_ok)
        def _():
            dn_copy(r, k).start()

        if ny == 2 and k in plain:
            y_copy(r, k).start()
    if ny == 2:
        mate = row_of(z, 1 - y)
        x_wait(mate, 0)

        @pl.when(above_ok)
        def _():
            up_copy(mate, 0).start()

        @pl.when(below_ok)
        def _():
            dn_copy(mate, 0).start()

    def relay(s, column, k, cross):
        @pl.when(z - s >= 0)
        def _():
            slot = row_of(z - s, column)
            x_wait(slot, k)

            @pl.when(above_ok)
            def _():
                up_copy(slot, k).start()

            if cross:
                y_copy(slot, k).start()

        @pl.when(z + s <= nz - 1)
        def _():
            slot = row_of(z + s, column)
            x_wait(slot, k)

            @pl.when(below_ok)
            def _():
                dn_copy(slot, k).start()

            if cross:
                y_copy(slot, k).start()

    load1.wait()

    @pl.loop(1, nz + 1)
    def _(s):
        @pl.when(s < nz)
        def _():
            for k in plain:
                relay(s, y, k, ny == 2)
            if ny == 2:
                relay(s, y, 0, False)
                relay(s, 1 - y, 0, False)

        each_at(s - 1, process)

        @pl.when(s - 2 < nz - 2)
        def _():
            each_at(s - 2, finish)

        @pl.when(s - 1 == nz - 2)
        def _():
            load2.wait()

        @pl.when(s - 1 >= nz - 2)
        def _():
            each_at(s - 1, finish)
            each_at(s - 1, project)

    def zd_copy(level, k):
        slot = jnp.where(z - 1 == level, nz, level)
        return z_copy(level, slot, k, row_of(z - 1, y))

    def zu_copy(level, k):
        return z_copy(level, level, k, row_of(z + 1, y))

    def z_copy(level, slot, k, device_row):
        if k == 3:
            src, dst = pout.at[row_of(level, 1 - y), :, cut[0]], zside.at[slot]
        else:
            src, dst = pout.at[row_of(level, y), :, cut[k]], zrecv.at[slot, :, cut[k]]
        return remote(src, dst, z_s.at[level, k], z_r.at[slot, k], {"row": device_row})

    def z_wait(slot, k):
        level = jnp.where(slot == nz, 0, slot)
        z_copy(level, slot, k, r).wait_recv()

    def incoming(slot, k):
        return zside[slot] if k == 3 else zrecv[slot, :, cut[k]]

    def reduce(level):
        inner = ((level < z) & above_ok) | ((level > z) & below_ok)
        order = (0, 3, 1, 2) if ny == 2 else plain
        for k in order:
            slot = row_of(level, 1 - y if k == 3 else y)
            where = cut[0] if k == 3 else cut[k]
            crossed = ny == 2 and k in plain
            if crossed:
                yp_copy(level, k).wait_recv()

            @pl.when(inner)
            def _():
                z_wait(level, k)
                total = pout[slot, :, where].astype(F32) + incoming(level, k).astype(F32)
                if crossed:
                    total += yrecv[level, :, where].astype(F32)
                pout[slot, :, where] = total.astype(BF16)

            if crossed:
                @pl.when(jnp.logical_not(inner))
                def _():
                    pout[slot, :, where] = (
                        pout[slot, :, where].astype(F32) + yrecv[level, :, where].astype(F32)
                    ).astype(BF16)

            @pl.when(level < z)
            def _():
                zd_copy(level, k).start()

            @pl.when(level > z)
            def _():
                zu_copy(level, k).start()

    @pl.loop(0, nz - 1)
    def _(i):
        each_at(nz - 3 - i, project)
        each_at(nz - 1 - i, reduce)

    def settle(k):
        slot = row_of(z, 1 - y) if k == 3 else r
        where = cut[0] if k == 3 else cut[k]
        acc[:, where] = pout[slot, :, where].astype(F32)

        @pl.when(below_ok)
        def _():
            z_wait(z, k)
            acc[:, where] += incoming(z, k).astype(F32)

        @pl.when(above_ok)
        def _():
            z_wait(nz, k)
            acc[:, where] += incoming(nz, k).astype(F32)

    if ny == 2:
        settle(3)
        pout[row_of(z, 1 - y), :, cut[0]] = acc[:, cut[0]].astype(BF16)
        yp_copy(z, 0).start()
    for k in (1, 2, 0):
        settle(k)
        total = acc[:, cut[k]] + dbias_ref[:, cut[k]]
        if ny == 2:
            yp_copy(z, k).wait_recv()
            total += yrecv[z, :, cut[k]].astype(F32)
        out_ref[:, cut[k]] = total.astype(BF16)

    @pl.loop(0, nz)
    def _(level):
        slots = [(row_of(level, y), k) for k in range(3)]
        if ny == 2:
            slots.append((row_of(level, 1 - y), 0))

        @pl.when((level <= z) & above_ok)
        def _():
            for slot, k in slots:
                up_copy(slot, k).wait_send()

        @pl.when((level >= z) & below_ok)
        def _():
            for slot, k in slots:
                dn_copy(slot, k).wait_send()

        if ny == 2:
            for k in plain:
                y_copy(row_of(level, y), k).wait_send()
                yp_copy(level, k).wait_send()
        p_copy(level).wait_send()

        @pl.when(level != z)
        def _():
            for k in range(4 if ny == 2 else 3):
                zu_copy(level, k).wait_send()

    if ny == 2:
        y_copy(r, 0).wait_send()
        yp_copy(z, 0).wait_send()


def solution(mesh):
    n_row = mesh.shape["row"]
    ny = 2 if n_row == 8 else 1
    nz = n_row // ny

    def on_device(tokens, norm_gain, norm_bias, up_weight, up_bias, down_weight, down_bias):
        t, dh = tokens.shape
        ff = up_weight.shape[1]
        dout = down_weight.shape[1]
        vmem = pl.BlockSpec(memory_space=pltpu.VMEM)
        hbm = pl.BlockSpec(memory_space=pl.ANY)
        dma = pltpu.SemaphoreType.DMA
        rows = ny * t
        return pl.pallas_call(
            functools.partial(kernel, nz, ny),
            out_shape=jax.ShapeDtypeStruct((t, dout), BF16),
            in_specs=[vmem, vmem, vmem, hbm, vmem, hbm, vmem],
            out_specs=vmem,
            scratch_shapes=[
                pltpu.VMEM((dh, ff), BF16),
                pltpu.VMEM((ff, dout), BF16),
                pltpu.VMEM((n_row, t, dh), BF16),
                pltpu.VMEM((nz, rows, ff), F32),
                pltpu.VMEM((nz, rows, ff), BF16),
                pltpu.VMEM((nz, rows, ff), BF16),
                pltpu.VMEM((nz, rows, ff), BF16),
                pltpu.VMEM((n_row, t, dout), BF16),
                pltpu.VMEM((nz if ny == 2 else 1, t, dout), BF16),
                pltpu.VMEM((nz + 1, t, dout), BF16),
                pltpu.VMEM((nz + 1 if ny == 2 else 1, t, dout // 6), BF16),
                pltpu.VMEM((t, dout), F32),
                pltpu.VMEM((2, t, 128), F32),
                pltpu.VMEM((2, t, 128), F32),
                dma((2,)), dma((2,)), dma((n_row, 3)),
                dma((n_row, 3)), dma((n_row, 3)), dma((n_row, 3)),
                dma((nz,)), dma((nz,)), dma((nz, 3)), dma((nz, 3)),
                dma((nz, 4)), dma((nz + 1, 4)),
            ],
            compiler_params=pltpu.CompilerParams(
                collective_id=0, has_side_effects=True, vmem_limit_bytes=62 * 1024 * 1024
            ),
            cost_estimate=pl.CostEstimate(
                flops=4 * n_row * t * dh * ff, bytes_accessed=4 * dh * ff, transcendentals=0
            ),
        )(
            tokens, norm_gain.reshape(1, -1), norm_bias.reshape(1, -1), up_weight,
            up_bias.reshape(1, -1), down_weight, down_bias.reshape(1, -1),
        )

    in_specs = (
        P(("groups", "row"), "col"),
        P("col"),
        P("col"),
        P("col", "row"),
        P("row"),
        P("row", "col"),
        P("col"),
    )
    out_specs = P(("groups", "row"), "col")
    return jax.shard_map(
        on_device, mesh=mesh, in_specs=in_specs, out_specs=out_specs, check_vma=False
    )
```
